32 devices in a mesh: seq: 16 (over z, y, x), head: 2 (over core).
Axes of the slice: x: 2, y: 2, z: 4, core: 2. Of those that a mesh axis runs over, the one named last changes fastest.
Arguments:
- queries: bfloat16 [2048, 4096], P('seq', 'head'), may hold values from -6 to 6
- keys: bfloat16 [2048, 4096], P('seq', 'head'), may hold values from -6 to 6
- values: bfloat16 [2048, 4096], P('seq', 'head'), may hold values from -6 to 6
- log_decay: float32 [2048, 32], P('seq', 'head'), may hold values from -0.75 to 0
- norm_gain: float32 [4096], P('head'), may hold values from 0.1 to 1.9
- out_weight: bfloat16 [4096, 4096], P('head'), may hold values from -0.125 to 0.125
- steer_ids: int32 [2048], P('seq'), may hold values from 0 to 15
- steer_table: bfloat16 [16, 4096], P(None, 'head'), may hold values from -3 to 3
Outputs:
- layer_out: bfloat16 [2048, 4096], P('seq', 'head')
The draws below stay inside these ranges and needn't reach their ends.
All inputs are finite; a program needn't handle non-finite values.
Results may differ from the reference program's by a relative error of at most 0.0052.
Values sent between devices are 32-bit elements; how exact they have to be, the bound alone decides.
A program may use at most 64 MiB of HBM per device.

```python
import math
import jax
import jax.numpy as jnp
from jax import lax

D = 4096
HEADS = 32
HEAD_DIM = 128
SPAN = 128
NSTEER = 16
TOKENS = 2048


def draw_log_decay(key, part):
    keys_all = jax.random.split(jax.random.fold_in(key, 7), 6)
    share = 0.5
    fast = jax.random.uniform(keys_all[0], (HEADS,)) < share
    fast_rate = -1.0 / jax.random.uniform(keys_all[1], (HEADS,), minval=30.0, maxval=50.0)
    slow_rate = math.log(0.7) / TOKENS * jax.random.uniform(keys_all[2], (HEADS,), minval=0.3, maxval=1.0)
    base = jnp.where(fast, fast_rate, slow_rate)
    rough = jax.random.uniform(keys_all[3], (TOKENS, HEADS), minval=0.5, maxval=1.5)
    spots = jax.random.randint(keys_all[4], (2,), 0, TOKENS)
    places = jnp.arange(TOKENS, dtype=jnp.int32)
    struck = jnp.any(places[:, None] == spots[None, :], axis=1)
    depth = jnp.log(jax.random.uniform(keys_all[5], (TOKENS, HEADS), minval=0.5, maxval=0.8))
    result = base[None, :] * rough + jnp.where(struck[:, None], depth, 0.0)
    return result.astype(jnp.float32)


def set_ends(entries, stream_key, smallest, top_value):
    index_at = [jax.random.randint(jax.random.fold_in(stream_key, axis), (), 0, length) for axis, length in enumerate(entries.shape)]
    main_axis = entries.shape.index(max(entries.shape))
    neighbour = index_at[:main_axis] + [(index_at[main_axis] + 1) % entries.shape[main_axis]] + index_at[main_axis + 1:]
    return entries.at[tuple(index_at)].set(smallest).at[tuple(neighbour)].set(top_value)


def with_spikes(values, key, source, target, blocks, factor):
    def block_of(axis_at):
        return (jnp.arange(values.shape[axis_at]) // (values.shape[axis_at] // blocks)).reshape((-1,) + (1,) * (values.ndim - 1 - axis_at))

    near = jax.random.permutation(key, blocks)[block_of(target)]
    far = (block_of(target) + blocks // 2) % blocks
    return jnp.where((block_of(source) == near) | (block_of(source) == far), factor * values, values)


def shard_levels(stream_key, shape, shards, low, top_value):
    def one(axis_at, blocks):
        draws = jax.random.uniform(jax.random.fold_in(jax.random.fold_in(stream_key, 6), axis_at), (blocks,), jnp.float32, low / len(shards), top_value / len(shards))
        return jnp.repeat(jnp.exp(draws), shape[axis_at] // blocks).reshape((-1,) + (1,) * (len(shape) - axis_at - 1))

    loudness = one(*shards[0])
    for cut in shards[1:]:
        loudness = loudness * one(*cut)
    return loudness


def gaussian(own_key, dims, width, limit, cuts=(), held_as=jnp.bfloat16):
    values = width * jax.random.normal(own_key, dims, jnp.float32)
    if cuts:
        values = values * shard_levels(own_key, dims, cuts, -0.22, 0.18)
    return jnp.clip(values, -limit, limit).astype(held_as)


def gaussian_with(key, dims, deviation, most, shards, heavy, held_as=jnp.bfloat16):
    values = deviation * jax.random.normal(key, dims, jnp.float32)
    if shards:
        values = values * shard_levels(key, dims, shards, -0.22, 0.18)
    return jnp.clip(with_spikes(values, jax.random.fold_in(key, 3), *heavy), -most, most).astype(held_as)


def setup_inputs(seed: int = 0) -> dict:
    key_of = jax.random.split(jax.random.key(seed), 9)
    queries = gaussian(key_of[0], (TOKENS, HEADS * HEAD_DIM), 1.0, 6.0, ((0, 16), (1, 2)))
    keys = gaussian(key_of[1], (TOKENS, HEADS * HEAD_DIM), 1.0, 6.0, ((0, 16), (1, 2)))
    values = gaussian(key_of[2], (TOKENS, HEADS * HEAD_DIM), 1.0, 6.0, ((0, 16), (1, 2)))
    log_decay = draw_log_decay(jax.random.fold_in(key_of[8], 71), 0)
    norm_gain = jnp.clip(1.0 + 0.18 * jax.random.normal(key_of[4], (HEADS * HEAD_DIM,), jnp.float32), 0.1, 1.9)
    out_weight = gaussian_with(key_of[5], (HEADS * HEAD_DIM, D), (HEADS * HEAD_DIM) ** -0.5, 0.125, ((0, 2),), (0, 1, 2, 2.0))
    steer_ids = set_ends(jax.random.randint(key_of[6], (TOKENS,), 0, NSTEER), jax.random.fold_in(key_of[6], 1), 0, NSTEER - 1).astype(jnp.int32)
    steer_table = gaussian(key_of[7], (NSTEER, D), 0.5, 3.0, ((1, 2),))
    return dict(queries=queries, keys=keys, values=values, log_decay=log_decay, norm_gain=norm_gain, out_weight=out_weight, steer_ids=steer_ids, steer_table=steer_table)


def block_step(state, inputs):
    query, key_blk, value_blk, decay = inputs
    cum = jnp.cumsum(decay, axis=1)
    size = decay.shape[1]
    rows = lax.broadcasted_iota(jnp.int32, (size, size), 0)
    cols = lax.broadcasted_iota(jnp.int32, (size, size), 1)
    lower = (cols <= rows)[None]
    scores = jnp.einsum('hte,hse->hts', query.astype(jnp.float32), key_blk.astype(jnp.float32))
    diffs = jnp.where(lower, cum[:, :, None] - cum[:, None, :], 0.0)
    block_weights = jnp.where(lower, jnp.exp(diffs), 0.0) * scores
    block_weights = block_weights.astype(jnp.bfloat16)
    intra = jnp.einsum('hts,hse->hte', block_weights.astype(jnp.float32), value_blk.astype(jnp.float32))
    inter = jnp.exp(cum)[:, :, None] * jnp.einsum('hte,hef->htf', query.astype(jnp.float32), state, precision=lax.Precision.HIGHEST)
    total = cum[:, -1]
    scaled_keys = key_blk.astype(jnp.float32) * jnp.exp(total[:, None] - cum)[:, :, None]
    update = jnp.einsum('hse,hsf->hef', scaled_keys, value_blk.astype(jnp.float32), precision=lax.Precision.HIGHEST)
    new_state = jnp.exp(total)[:, None, None] * state + update
    return (new_state, intra + inter)

def reference(queries, keys, values, log_decay, norm_gain, out_weight, steer_ids, steer_table):
    count = TOKENS // SPAN

    def split(array):
        return array.reshape(count, SPAN, HEADS, HEAD_DIM).transpose(0, 2, 1, 3)
    decays = log_decay.reshape(count, SPAN, HEADS).transpose(0, 2, 1)
    start = jnp.zeros((HEADS, HEAD_DIM, HEAD_DIM), jnp.float32)
    final, blocks = lax.scan(block_step, start, (split(queries), split(keys), split(values), decays))
    attended = blocks.transpose(0, 2, 1, 3).reshape(TOKENS, HEADS, HEAD_DIM)
    mean_sq = lax.optimization_barrier(jnp.mean(attended * attended, axis=-1, keepdims=True))
    normed = (attended * lax.rsqrt(mean_sq + 1e-06)).reshape(TOKENS, HEADS * HEAD_DIM) * norm_gain
    normed = normed.astype(jnp.bfloat16)
    projected = jnp.dot(normed, out_weight, preferred_element_type=jnp.float32)
    onehot = (steer_ids[:, None] == jnp.arange(NSTEER, dtype=jnp.int32)[None, :]).astype(jnp.bfloat16)
    steering = jnp.dot(onehot, steer_table, preferred_element_type=jnp.float32)
    return (projected + steering).astype(jnp.bfloat16)
```

```python
import functools

import jax
import jax.numpy as jnp
from jax import lax
from jax.experimental import pallas as pl
from jax.experimental.pallas import tpu as pltpu
from jax.sharding import PartitionSpec as P

MESH = pl.DeviceIdType.MESH
F32 = jnp.float32
BF16 = jnp.bfloat16
W_COPIES = 8


def split_high_low(x):
    high = x.astype(BF16)
    return high, (x - high.astype(F32)).astype(BF16)


def kernel(
    n, nh, G, SUB, hb, nt,
    q_ref, k_ref, v_ref, ld_ref, gain_ref, w_hbm, ids_ref, tab_ref,
    out_ref,
    w_ref, mem_own, dec_own, mem_in, dec_in, chain_out, chain_in, pre_out, pre_in,
    intra, ecb, acc, xout, xin,
    w_sem, mem_s, mem_r, dec_s, dec_r, ch_s, ch_r, pre_s, pre_r, x_s, x_r,
):
    T, features = q_ref.shape
    HD = 128
    heads = features // HD
    HS = heads // G
    NG = n // G
    width = w_hbm.shape[1]
    CW = width // nh
    TW = CW // nt
    s = lax.axis_index("seq")
    e = lax.axis_index("head")
    g = s // G
    c = s % G

    def member(o):
        return (c + o) % G

    barrier = pltpu.get_barrier_semaphore()
    for o in range(1, G):
        pl.semaphore_signal(barrier, 1, device_id=(g * G + member(o), e), device_id_type=MESH)
    for o in range(1, nh):
        pl.semaphore_signal(barrier, 1, device_id=(s, (e + o) % nh), device_id_type=MESH)

    @pl.when(g > 0)
    def _():
        pl.semaphore_signal(barrier, 1, device_id=(s - G, e), device_id_type=MESH)

    @pl.when(g < NG - 1)
    def _():
        pl.semaphore_signal(barrier, 1, device_id=(s + G, e), device_id_type=MESH)

    wr = features // W_COPIES
    w_copies = [
        pltpu.make_async_copy(
            w_hbm.at[pl.ds(i * wr, wr)], w_ref.at[pl.ds(i * wr, wr)], w_sem.at[i]
        )
        for i in range(W_COPIES)
    ]

    ld = ld_ref[...]
    rows = lax.broadcasted_iota(jnp.int32, (T, T), 0)
    cols = lax.broadcasted_iota(jnp.int32, (T, T), 1)
    lower = cols <= rows
    tril = jnp.where(lower, 1.0, 0.0).astype(F32)
    cum = jnp.dot(tril, ld, precision=lax.Precision.HIGHEST, preferred_element_type=F32)
    cum_row = lax.dot_general(
        ld, tril, (((0,), (1,)), ((), ())),
        precision=lax.Precision.HIGHEST, preferred_element_type=F32,
    )
    total_row = cum[T - 1 : T, :]
    key_w = jnp.exp(total_row - cum)
    grow = jnp.exp(cum)
    block_decay = jnp.broadcast_to(jnp.exp(cum_row[:, T - 1 : T]), (heads, HD))
    pad = dec_own.shape[1]
    for j in range(G):
        part = block_decay[j * HS : (j + 1) * HS, :]
        if pad > HS:
            part = jnp.concatenate([part, jnp.zeros((pad - HS, HD), F32)], axis=0)
        dec_own[j] = part

    def dec_copy(to, frm):
        return pltpu.make_async_remote_copy(
            src_ref=dec_own.at[to], dst_ref=dec_in.at[frm],
            send_sem=dec_s.at[to], recv_sem=dec_r.at[frm],
            device_id=(g * G + to, e), device_id_type=MESH,
        )

    def mem_copy(to, frm, u):
        return pltpu.make_async_remote_copy(
            src_ref=mem_own.at[to, u], dst_ref=mem_in.at[frm, u],
            send_sem=mem_s.at[to, u], recv_sem=mem_r.at[frm, u],
            device_id=(g * G + to, e), device_id_type=MESH,
        )

    def pre_copy(to, frm, u):
        return pltpu.make_async_remote_copy(
            src_ref=pre_out.at[to, u], dst_ref=pre_in.at[frm, u],
            send_sem=pre_s.at[to, u], recv_sem=pre_r.at[frm, u],
            device_id=(g * G + to, e), device_id_type=MESH,
        )

    def chain_copy(u):
        return pltpu.make_async_remote_copy(
            src_ref=chain_out.at[u], dst_ref=chain_in.at[u],
            send_sem=ch_s.at[u], recv_sem=ch_r.at[u],
            device_id=((s + G) % n, e), device_id_type=MESH,
        )

    for u in range(SUB):
        for j in range(G):
            for r in range(hb):
                h = j * HS + u * hb + r
                lanes = slice(h * HD, (h + 1) * HD)
                high, low = split_high_low(k_ref[:, lanes].astype(F32) * key_w[:, h : h + 1])
                value = v_ref[:, lanes]
                mem_own[j, u, r] = lax.dot_general(
                    jnp.concatenate([high, low], axis=0),
                    jnp.concatenate([value, value], axis=0),
                    (((0,), (0,)), ((), ())),
                    preferred_element_type=F32,
                )
        if u == 0:
            beside = (g + NG - 1) // NG + (2 * NG - 2 - g) // NG
            pl.semaphore_wait(barrier, (G - 1) + (nh - 1) + beside)
            for o in range(1, G):
                dec_copy(member(o), c).start()
        for o in range(1, G):
            mem_copy(member(o), c, u).start()
        mem_in[c, u] = mem_own[c, u]
    dec_in[c] = dec_own[c]
    for copy in w_copies:
        copy.start()

    for h in range(heads):
        lanes = slice(h * HD, (h + 1) * HD)
        scores = lax.dot_general(
            q_ref[:, lanes], k_ref[:, lanes], (((1,), (1,)), ((), ())),
            preferred_element_type=F32,
        )
        diffs = jnp.where(lower, cum[:, h : h + 1] - cum_row[h : h + 1, :], 0.0)
        weights = (jnp.where(lower, jnp.exp(diffs), 0.0) * scores).astype(BF16)
        intra[h] = jnp.dot(weights, v_ref[:, lanes], preferred_element_type=F32)
        ecb[h] = jnp.broadcast_to(grow[:, h : h + 1], (T, HD))
    nsteer = tab_ref.shape[0]
    ids = jnp.broadcast_to(ids_ref[...], (nsteer, T))
    onehot = jnp.where(ids == lax.broadcasted_iota(jnp.int32, (nsteer, T), 0), 1.0, 0.0).astype(BF16)
    acc[...] = jnp.zeros_like(acc)
    acc[:, pl.ds(pl.multiple_of(e * CW, CW), CW)] = lax.dot_general(
        onehot, tab_ref[...], (((0,), (0,)), ((), ())), preferred_element_type=F32
    )

    for o in range(1, G):
        dec_copy(c, member(o)).wait_recv()
    for u in range(SUB):
        for o in range(1, G):
            mem_copy(c, member(o), u).wait_recv()

        @pl.when(g > 0)
        def _():
            chain_copy(u).wait_recv()

        @pl.when(g == 0)
        def _():
            chain_in[u] = jnp.zeros(chain_in.shape[1:], F32)

        for r in range(hb):
            state = chain_in[u, r]
            row = u * hb + r
            for j in range(G):
                pre_out[j, u, r] = state
                state = state * dec_in[j, row : row + 1, :] + mem_in[j, u, r]
            chain_out[u, r] = state

        @pl.when(g < NG - 1)
        def _():
            chain_copy(u).start()

        for o in range(1, G):
            pre_copy(member(o), c, u).start()
        pre_in[c, u] = pre_out[c, u]

    def normed_chunk(j, u):
        parts = []
        for r in range(hb):
            h = j * HS + u * hb + r
            lanes = pl.ds(pl.multiple_of(h * HD, HD), HD)
            high, low = split_high_low(pre_in[j, u, r])
            query = q_ref[:, lanes]
            carried = jnp.dot(
                jnp.concatenate([query, query], axis=1),
                jnp.concatenate([high, low], axis=0),
                preferred_element_type=F32,
            )
            attended = intra[h] + ecb[h] * carried
            mean_sq = jnp.mean(attended * attended, axis=1, keepdims=True)
            normed = attended * lax.rsqrt(mean_sq + 1e-6) * gain_ref[:, lanes]
            parts.append(normed.astype(BF16))
        return parts[0] if hb == 1 else jnp.concatenate(parts, axis=1)

    def w_rows(j, u):
        return pl.ds(pl.multiple_of((j * HS + u * hb) * HD, HD), hb * HD)

    for copy in w_copies:
        copy.wait()

    def step(i, carry):
        u, o = i // G, i % G
        j = (c + o) % G

        @pl.when(o > 0)
        def _():
            pre_copy(c, j, u).wait_recv()

        chunk = normed_chunk(j, u)
        for t in range(width // TW):
            at = slice(t * TW, (t + 1) * TW)
            acc[:, at] += jnp.dot(chunk, w_ref[w_rows(j, u), at], preferred_element_type=F32)
        return carry

    lax.fori_loop(0, G * SUB - 1, step, 0)

    last = (c + G - 1) % G
    pre_copy(c, last, SUB - 1).wait_recv()
    chunk = normed_chunk(last, SUB - 1)
    rows_last = w_rows(last, SUB - 1)

    def x_copy(o, t):
        return pltpu.make_async_remote_copy(
            src_ref=xout.at[o - 1, t], dst_ref=xin.at[o - 1, t],
            send_sem=x_s.at[o - 1, t], recv_sem=x_r.at[o - 1, t],
            device_id=(s, (e + o) % nh), device_id_type=MESH,
        )

    for o in range(1, nh):
        to = (e + o) % nh
        for t in range(nt):
            at = pl.ds(pl.multiple_of(to * CW + t * TW, TW), TW)
            xout[o - 1, t] = acc[:, at] + jnp.dot(
                chunk, w_ref[rows_last, at], preferred_element_type=F32
            )
            x_copy(o, t).start()
    for t in range(nt):
        at = pl.ds(pl.multiple_of(e * CW + t * TW, TW), TW)
        acc[:, at] += jnp.dot(chunk, w_ref[rows_last, at], preferred_element_type=F32)
    for t in range(nt):
        at = pl.ds(pl.multiple_of(e * CW + t * TW, TW), TW)
        whole = acc[:, at]
        for o in range(1, nh):
            x_copy(o, t).wait_recv()
            whole = whole + xin[o - 1, t]
        out_ref[:, t * TW : (t + 1) * TW] = whole.astype(BF16)

    for o in range(1, G):
        dec_copy(member(o), c).wait_send()
        for u in range(SUB):
            mem_copy(member(o), c, u).wait_send()
            pre_copy(member(o), c, u).wait_send()
    for o in range(1, nh):
        for t in range(nt):
            x_copy(o, t).wait_send()

    @pl.when(g < NG - 1)
    def _():
        for u in range(SUB):
            chain_copy(u).wait_send()


def solution(mesh):
    n, nh = mesh.shape["seq"], mesh.shape["head"]

    def shards(queries, keys, values, log_decay, norm_gain, out_weight, steer_ids, steer_table):
        T, features = queries.shape
        heads = log_decay.shape[1]
        HD = features // heads
        width = out_weight.shape[1]
        CW = width // nh
        G = 4
        HS = heads // G
        hb = 2 if HS % 2 == 0 else 1
        SUB = HS // hb
        nt = max(1, CW // 512)
        TW = CW // nt
        pad = (HS + 7) // 8 * 8
        DMA = pltpu.SemaphoreType.DMA
        vmem = pl.BlockSpec(memory_space=pltpu.VMEM)
        return pl.pallas_call(
            functools.partial(kernel, n, nh, G, SUB, hb, nt),
            out_shape=jax.ShapeDtypeStruct((T, CW), BF16),
            in_specs=[vmem] * 5 + [pl.BlockSpec(memory_space=pl.ANY)] + [vmem] * 2,
            out_specs=vmem,
            scratch_shapes=[
                pltpu.VMEM((features, width), BF16),
                pltpu.VMEM((G, SUB, hb, HD, HD), F32),
                pltpu.VMEM((G, pad, HD), F32),
                pltpu.VMEM((G, SUB, hb, HD, HD), F32),
                pltpu.VMEM((G, pad, HD), F32),
                pltpu.VMEM((SUB, hb, HD, HD), F32),
                pltpu.VMEM((SUB, hb, HD, HD), F32),
                pltpu.VMEM((G, SUB, hb, HD, HD), F32),
                pltpu.VMEM((G, SUB, hb, HD, HD), F32),
                pltpu.VMEM((heads, T, HD), F32),
                pltpu.VMEM((heads, T, HD), F32),
                pltpu.VMEM((T, width), F32),
                pltpu.VMEM((nh - 1, nt, T, TW), F32),
                pltpu.VMEM((nh - 1, nt, T, TW), F32),
                DMA((W_COPIES,)),
                DMA((G, SUB)), DMA((G, SUB)),
                DMA((G,)), DMA((G,)),
                DMA((SUB,)), DMA((SUB,)),
                DMA((G, SUB)), DMA((G, SUB)),
                DMA((nh - 1, nt)), DMA((nh - 1, nt)),
            ],
            compiler_params=pltpu.CompilerParams(
                collective_id=0, has_side_effects=True, vmem_limit_bytes=52 * 1024 * 1024
            ),
            cost_estimate=pl.CostEstimate(
                flops=2 * T * features * width,
                bytes_accessed=2 * features * width,
                transcendentals=T * T * heads,
            ),
        )(
            queries, keys, values, log_decay, norm_gain.reshape(1, features), out_weight,
            steer_ids.reshape(1, T), steer_table,
        )

    in_specs = (
        P("seq", "head"), P("seq", "head"), P("seq", "head"), P("seq", "head"),
        P("head"), P("head", None), P("seq"), P(None, "head"),
    )
    return jax.shard_map(
        shards, mesh=mesh, in_specs=in_specs, out_specs=P("seq", "head"), check_vma=False
    )
```

```python
import functools

import jax
import jax.numpy as jnp
from jax import lax
from jax.experimental import pallas as pl
from jax.experimental.pallas import tpu as pltpu
from jax.sharding import PartitionSpec as P

MESH = pl.DeviceIdType.MESH
F32 = jnp.float32
BF16 = jnp.bfloat16
W_COPIES = 8


def split_high_low(x):
    high = x.astype(BF16)
    return high, (x - high.astype(F32)).astype(BF16)


def kernel(
    n, nh, G, SUB, hb, nt,
    q_hbm, k_hbm, v_hbm, ld_hbm, gain_hbm, w_hbm, ids_hbm, tab_hbm,
    out_ref,
    q_ref, k_ref, v_ref, ld_ref, gain_ref, ids_ref, tab_ref, in_sem,
    w_ref, mem_own, dec_own, mem_in, dec_in, chain_out, chain_in, pre_out, pre_in,
    intra, ecb, acc, xout, xin,
    w_sem, mem_s, mem_r, dec_s, dec_r, ch_s, ch_r, pre_s, pre_r, x_s, x_r,
):
    T, features = q_hbm.shape
    HD = 128
    heads = features // HD
    HS = heads // G
    NG = n // G
    width = w_hbm.shape[1]
    CW = width // nh
    TW = CW // nt
    s = lax.axis_index("seq")
    e = lax.axis_index("head")
    g = s // G
    c = s % G

    def member(i):
        o, bit, rank = (G - i) % G, 1, 0
        while bit < G:
            rank = rank + (c // bit + o // bit) % 2 * bit
            bit *= 2
        return rank

    fetch_ld, fetch_k, fetch_v, fetch_q, fetch_gain, fetch_ids, fetch_tab = [
        pltpu.make_async_copy(src, dst, in_sem.at[i])
        for i, (src, dst) in enumerate(
            [
                (ld_hbm, ld_ref), (k_hbm, k_ref), (v_hbm, v_ref), (q_hbm, q_ref),
                (gain_hbm, gain_ref), (ids_hbm, ids_ref), (tab_hbm, tab_ref),
            ]
        )
    ]
    for copy in (fetch_ld, fetch_k, fetch_v, fetch_q, fetch_gain, fetch_ids, fetch_tab):
        copy.start()

    barrier = pltpu.get_barrier_semaphore()
    for o in range(1, G):
        pl.semaphore_signal(barrier, 1, device_id=(g * G + member(o), e), device_id_type=MESH)
    for o in range(1, nh):
        pl.semaphore_signal(barrier, 1, device_id=(s, (e + o) % nh), device_id_type=MESH)

    @pl.when(g > 0)
    def _():
        pl.semaphore_signal(barrier, 1, device_id=(s - G, e), device_id_type=MESH)

    @pl.when(g < NG - 1)
    def _():
        pl.semaphore_signal(barrier, 1, device_id=(s + G, e), device_id_type=MESH)

    wr = features // W_COPIES
    w_copies = [
        pltpu.make_async_copy(
            w_hbm.at[pl.ds(i * wr, wr)], w_ref.at[pl.ds(i * wr, wr)], w_sem.at[i]
        )
        for i in range(W_COPIES)
    ]

    fetch_ld.wait()
    ld = ld_ref[...]
    rows = lax.broadcasted_iota(jnp.int32, (T, T), 0)
    cols = lax.broadcasted_iota(jnp.int32, (T, T), 1)
    lower = cols <= rows
    tril = jnp.where(lower, 1.0, 0.0).astype(F32)
    cum = lax.dot_general(
        tril, ld, (((1,), (1,)), ((), ())),
        precision=lax.Precision.HIGHEST, preferred_element_type=F32,
    )
    cum_row = lax.dot_general(
        ld, tril, (((1,), (1,)), ((), ())),
        precision=lax.Precision.HIGHEST, preferred_element_type=F32,
    )
    total_row = cum[T - 1 : T, :]
    key_w = jnp.exp(total_row - cum)
    grow = jnp.exp(cum)
    block_decay = jnp.broadcast_to(jnp.exp(cum_row[:, T - 1 : T]), (heads, HD))
    pad = dec_own.shape[1]
    for j in range(G):
        part = block_decay[j * HS : (j + 1) * HS, :]
        if pad > HS:
            part = jnp.concatenate([part, jnp.zeros((pad - HS, HD), F32)], axis=0)
        dec_own[j] = part

    def dec_copy(to, frm):
        return pltpu.make_async_remote_copy(
            src_ref=dec_own.at[to], dst_ref=dec_in.at[frm],
            send_sem=dec_s.at[to], recv_sem=dec_r.at[frm],
            device_id=(g * G + to, e), device_id_type=MESH,
        )

    def mem_copy(to, frm, u):
        return pltpu.make_async_remote_copy(
            src_ref=mem_own.at[to, u], dst_ref=mem_in.at[frm, u],
            send_sem=mem_s.at[to, u], recv_sem=mem_r.at[frm, u],
            device_id=(g * G + to, e), device_id_type=MESH,
        )

    def pre_copy(to, frm, u):
        return pltpu.make_async_remote_copy(
            src_ref=pre_out.at[to, u], dst_ref=pre_in.at[frm, u],
            send_sem=pre_s.at[to, u], recv_sem=pre_r.at[frm, u],
            device_id=(g * G + to, e), device_id_type=MESH,
        )

    def chain_copy(u):
        return pltpu.make_async_remote_copy(
            src_ref=chain_out.at[u], dst_ref=chain_in.at[u],
            send_sem=ch_s.at[u], recv_sem=ch_r.at[u],
            device_id=((s + G) % n, e), device_id_type=MESH,
        )

    fetch_k.wait()
    fetch_v.wait()
    for u in range(SUB):
        for j in range(G):
            for r in range(hb):
                h = j * HS + u * hb + r
                lanes = slice(h * HD, (h + 1) * HD)
                high, low = split_high_low(k_ref[:, lanes].astype(F32) * key_w[:, h : h + 1])
                value = v_ref[:, lanes]
                mem_own[j, u, r] = lax.dot_general(
                    jnp.concatenate([high, low], axis=0),
                    jnp.concatenate([value, value], axis=0),
                    (((0,), (0,)), ((), ())),
                    preferred_element_type=F32,
                )
        if u == 0:
            beside = (g + NG - 1) // NG + (2 * NG - 2 - g) // NG
            pl.semaphore_wait(barrier, (G - 1) + (nh - 1) + beside)
            for o in range(1, G):
                dec_copy(member(o), c).start()
        for o in range(1, G):
            mem_copy(member(o), c, u).start()
        mem_in[c, u] = mem_own[c, u]
    dec_in[c] = dec_own[c]
    for copy in w_copies:
        copy.start()

    for copy in (fetch_q, fetch_gain, fetch_ids, fetch_tab):
        copy.wait()
    for h in range(heads):
        lanes = slice(h * HD, (h + 1) * HD)
        scores = lax.dot_general(
            q_ref[:, lanes], k_ref[:, lanes], (((1,), (1,)), ((), ())),
            preferred_element_type=F32,
        )
        diffs = jnp.where(lower, cum[:, h : h + 1] - cum_row[h : h + 1, :], 0.0)
        weights = (jnp.where(lower, jnp.exp(diffs), 0.0) * scores).astype(BF16)
        intra[h] = jnp.dot(weights, v_ref[:, lanes], preferred_element_type=F32)
        ecb[h] = jnp.broadcast_to(grow[:, h : h + 1], (T, HD))
    nsteer = tab_ref.shape[0]
    ids = jnp.broadcast_to(ids_ref[...], (nsteer, T))
    onehot = jnp.where(ids == lax.broadcasted_iota(jnp.int32, (nsteer, T), 0), 1.0, 0.0).astype(BF16)
    acc[...] = jnp.zeros_like(acc)
    acc[:, pl.ds(pl.multiple_of(e * CW, CW), CW)] = lax.dot_general(
        onehot, tab_ref[...], (((0,), (0,)), ((), ())), preferred_element_type=F32
    )

    for o in range(1, G):
        dec_copy(c, member(o)).wait_recv()
    for u in range(SUB):
        for o in range(1, G):
            mem_copy(c, member(o), u).wait_recv()

        @pl.when(g > 0)
        def _():
            chain_copy(u).wait_recv()

        @pl.when(g == 0)
        def _():
            chain_in[u] = jnp.zeros(chain_in.shape[1:], F32)

        for r in range(hb):
            state = chain_in[u, r]
            row = u * hb + r
            for j in range(G):
                pre_out[j, u, r] = state
                state = state * dec_in[j, row : row + 1, :] + mem_in[j, u, r]
            chain_out[u, r] = state

        @pl.when(g < NG - 1)
        def _():
            chain_copy(u).start()

        for o in range(1, G):
            pre_copy(member(o), c, u).start()
        pre_in[c, u] = pre_out[c, u]

    def normed_chunk(j, u):
        parts = []
        for r in range(hb):
            h = j * HS + u * hb + r
            lanes = pl.ds(pl.multiple_of(h * HD, HD), HD)
            high, low = split_high_low(pre_in[j, u, r])
            query = q_ref[:, lanes]
            carried = jnp.dot(
                jnp.concatenate([query, query], axis=1),
                jnp.concatenate([high, low], axis=0),
                preferred_element_type=F32,
            )
            attended = intra[h] + ecb[h] * carried
            mean_sq = jnp.mean(attended * attended, axis=1, keepdims=True)
            normed = attended * lax.rsqrt(mean_sq + 1e-6) * gain_ref[:, lanes]
            parts.append(normed.astype(BF16))
        return parts[0] if hb == 1 else jnp.concatenate(parts, axis=1)

    def w_rows(j, u):
        return pl.ds(pl.multiple_of((j * HS + u * hb) * HD, HD), hb * HD)

    for copy in w_copies:
        copy.wait()

    def step(i, carry):
        u, o = i // G, i % G
        j = member(o)

        @pl.when(o > 0)
        def _():
            pre_copy(c, j, u).wait_recv()

        chunk = normed_chunk(j, u)
        for t in range(width // TW):
            at = slice(t * TW, (t + 1) * TW)
            acc[:, at] += jnp.dot(chunk, w_ref[w_rows(j, u), at], preferred_element_type=F32)
        return carry

    lax.fori_loop(0, G * SUB - 1, step, 0)

    last = member(G - 1)
    pre_copy(c, last, SUB - 1).wait_recv()
    chunk = normed_chunk(last, SUB - 1)
    rows_last = w_rows(last, SUB - 1)

    def x_copy(o, t):
        return pltpu.make_async_remote_copy(
            src_ref=xout.at[o - 1, t], dst_ref=xin.at[o - 1, t],
            send_sem=x_s.at[o - 1, t], recv_sem=x_r.at[o - 1, t],
            device_id=(s, (e + o) % nh), device_id_type=MESH,
        )

    for o in range(1, nh):
        to = (e + o) % nh
        for t in range(nt):
            at = pl.ds(pl.multiple_of(to * CW + t * TW, TW), TW)
            xout[o - 1, t] = acc[:, at] + jnp.dot(
                chunk, w_ref[rows_last, at], preferred_element_type=F32
            )
            x_copy(o, t).start()
    for t in range(nt):
        at = pl.ds(pl.multiple_of(e * CW + t * TW, TW), TW)
        acc[:, at] += jnp.dot(chunk, w_ref[rows_last, at], preferred_element_type=F32)
    for t in range(nt):
        at = pl.ds(pl.multiple_of(e * CW + t * TW, TW), TW)
        whole = acc[:, at]
        for o in range(1, nh):
            x_copy(o, t).wait_recv()
            whole = whole + xin[o - 1, t]
        out_ref[:, t * TW : (t + 1) * TW] = whole.astype(BF16)

    for o in range(1, G):
        dec_copy(member(o), c).wait_send()
        for u in range(SUB):
            mem_copy(member(o), c, u).wait_send()
            pre_copy(member(o), c, u).wait_send()
    for o in range(1, nh):
        for t in range(nt):
            x_copy(o, t).wait_send()

    @pl.when(g < NG - 1)
    def _():
        for u in range(SUB):
            chain_copy(u).wait_send()


def solution(mesh):
    n, nh = mesh.shape["seq"], mesh.shape["head"]

    def shards(queries, keys, values, log_decay, norm_gain, out_weight, steer_ids, steer_table):
        T, features = queries.shape
        heads = log_decay.shape[1]
        HD = features // heads
        width = out_weight.shape[1]
        CW = width // nh
        G = 8 if heads % 8 == 0 else 4
        HS = heads // G
        hb = 1
        SUB = HS // hb
        nt = max(1, CW // 512)
        TW = CW // nt
        pad = (HS + 7) // 8 * 8
        DMA = pltpu.SemaphoreType.DMA
        return pl.pallas_call(
            functools.partial(kernel, n, nh, G, SUB, hb, nt),
            out_shape=jax.ShapeDtypeStruct((T, CW), BF16),
            in_specs=[pl.BlockSpec(memory_space=pltpu.HBM)] * 8,
            out_specs=pl.BlockSpec(memory_space=pltpu.VMEM),
            scratch_shapes=[
                pltpu.VMEM((T, features), BF16),
                pltpu.VMEM((T, features), BF16),
                pltpu.VMEM((T, features), BF16),
                pltpu.VMEM((heads, T), F32),
                pltpu.VMEM((1, features), F32),
                pltpu.VMEM((1, T), jnp.int32),
                pltpu.VMEM(steer_table.shape, BF16),
                DMA((7,)),
                pltpu.VMEM((features, width), BF16),
                pltpu.VMEM((G, SUB, hb, HD, HD), F32),
                pltpu.VMEM((G, pad, HD), F32),
                pltpu.VMEM((G, SUB, hb, HD, HD), F32),
                pltpu.VMEM((G, pad, HD), F32),
                pltpu.VMEM((SUB, hb, HD, HD), F32),
                pltpu.VMEM((SUB, hb, HD, HD), F32),
                pltpu.VMEM((G, SUB, hb, HD, HD), F32),
                pltpu.VMEM((G, SUB, hb, HD, HD), F32),
                pltpu.VMEM((heads, T, HD), F32),
                pltpu.VMEM((heads, T, HD), F32),
                pltpu.VMEM((T, width), F32),
                pltpu.VMEM((nh - 1, nt, T, TW), F32),
                pltpu.VMEM((nh - 1, nt, T, TW), F32),
                DMA((W_COPIES,)),
                DMA((G, SUB)), DMA((G, SUB)),
                DMA((G,)), DMA((G,)),
                DMA((SUB,)), DMA((SUB,)),
                DMA((G, SUB)), DMA((G, SUB)),
                DMA((nh - 1, nt)), DMA((nh - 1, nt)),
            ],
            compiler_params=pltpu.CompilerParams(
                collective_id=0, has_side_effects=True, vmem_limit_bytes=52 * 1024 * 1024
            ),
            cost_estimate=pl.CostEstimate(
                flops=2 * T * features * width,
                bytes_accessed=2 * features * width,
                transcendentals=T * T * heads,
            ),
        )(
            queries, keys, values, log_decay.T, norm_gain.reshape(1, features), out_weight,
            steer_ids.reshape(1, T), steer_table,
        )

    in_specs = (
        P("seq", "head"), P("seq", "head"), P("seq", "head"), P("seq", "head"),
        P("head"), P("head", None), P("seq"), P(None, "head"),
    )
    return jax.shard_map(
        shards, mesh=mesh, in_specs=in_specs, out_specs=P("seq", "head"), check_vma=False
    )
```

```python
import functools

import jax
import jax.numpy as jnp
from jax import lax
from jax.experimental import pallas as pl
from jax.experimental.pallas import tpu as pltpu
from jax.sharding import PartitionSpec as P

MESH = pl.DeviceIdType.MESH
F32 = jnp.float32
BF16 = jnp.bfloat16
W_COPIES = 8


def split_high_low(x):
    high = x.astype(BF16)
    return high, (x - high.astype(F32)).astype(BF16)


def kernel(
    n, nh, G, SUB, hb, nt,
    q_hbm, k_hbm, v_hbm, ld_hbm, gain_hbm, w_hbm, ids_hbm, tab_hbm,
    out_ref,
    q_ref, k_ref, v_ref, ld_ref, gain_ref, ids_ref, tab_ref, in_sem,
    w_ref, mem_own, dec_own, mem_in, dec_in, chain_out, chain_in, pre_out, pre_in,
    intra, ecb, acc, xout, xin,
    w_sem, mem_s, mem_r, dec_s, dec_r, ch_s, ch_r, pre_s, pre_r, x_s, x_r,
):
    T, features = q_hbm.shape
    HD = 128
    heads = features // HD
    HS = heads // G
    NG = n // G
    width = w_hbm.shape[1]
    CW = width // nh
    TW = CW // nt
    s = lax.axis_index("seq")
    e = lax.axis_index("head")
    g = s // G
    c = s % G

    def member(i):
        o, bit, rank = (G - i) % G, 1, 0
        while bit < G:
            rank = rank + (c // bit + o // bit) % 2 * bit
            bit *= 2
        return rank

    fetch_ld, fetch_k, fetch_v, fetch_q, fetch_gain, fetch_ids, fetch_tab = [
        pltpu.make_async_copy(src, dst, in_sem.at[i])
        for i, (src, dst) in enumerate(
            [
                (ld_hbm, ld_ref), (k_hbm, k_ref), (v_hbm, v_ref), (q_hbm, q_ref),
                (gain_hbm, gain_ref), (ids_hbm, ids_ref), (tab_hbm, tab_ref),
            ]
        )
    ]
    for copy in (fetch_ld, fetch_k, fetch_v, fetch_q, fetch_gain, fetch_ids, fetch_tab):
        copy.start()

    barrier = pltpu.get_barrier_semaphore()
    for o in range(1, G):
        pl.semaphore_signal(barrier, 1, device_id=(g * G + member(o), e), device_id_type=MESH)
    for o in range(1, nh):
        pl.semaphore_signal(barrier, 1, device_id=(s, (e + o) % nh), device_id_type=MESH)

    @pl.when(g > 0)
    def _():
        pl.semaphore_signal(barrier, 1, device_id=(s - G, e), device_id_type=MESH)

    @pl.when(g < NG - 1)
    def _():
        pl.semaphore_signal(barrier, 1, device_id=(s + G, e), device_id_type=MESH)

    wr = features // W_COPIES
    w_copies = [
        pltpu.make_async_copy(
            w_hbm.at[pl.ds(i * wr, wr)], w_ref.at[pl.ds(i * wr, wr)], w_sem.at[i]
        )
        for i in range(W_COPIES)
    ]

    fetch_ld.wait()
    ld = ld_ref[...]
    rows = lax.broadcasted_iota(jnp.int32, (T, T), 0)
    cols = lax.broadcasted_iota(jnp.int32, (T, T), 1)
    lower = cols <= rows
    tril = jnp.where(lower, 1.0, 0.0).astype(F32)
    cum = lax.dot_general(
        tril, ld, (((1,), (1,)), ((), ())),
        precision=lax.Precision.HIGHEST, preferred_element_type=F32,
    )
    cum_row = lax.dot_general(
        ld, tril, (((1,), (1,)), ((), ())),
        precision=lax.Precision.HIGHEST, preferred_element_type=F32,
    )
    total_row = cum[T - 1 : T, :]
    key_w = jnp.exp(total_row - cum)
    grow = jnp.exp(cum)
    block_decay = jnp.broadcast_to(jnp.exp(cum_row[:, T - 1 : T]), (heads, HD))
    pad = dec_own.shape[1]
    for j in range(G):
        part = block_decay[j * HS : (j + 1) * HS, :]
        if pad > HS:
            part = jnp.concatenate([part, jnp.zeros((pad - HS, HD), F32)], axis=0)
        dec_own[j] = part

    def dec_copy(to, frm):
        return pltpu.make_async_remote_copy(
            src_ref=dec_own.at[to], dst_ref=dec_in.at[frm],
            send_sem=dec_s.at[to], recv_sem=dec_r.at[frm],
            device_id=(g * G + to, e), device_id_type=MESH,
        )

    def mem_copy(to, frm, u):
        return pltpu.make_async_remote_copy(
            src_ref=mem_own.at[to, u], dst_ref=mem_in.at[frm, u],
            send_sem=mem_s.at[to, u], recv_sem=mem_r.at[frm, u],
            device_id=(g * G + to, e), device_id_type=MESH,
        )

    def pre_copy(to, frm, u):
        return pltpu.make_async_remote_copy(
            src_ref=pre_out.at[to, u], dst_ref=pre_in.at[frm, u],
            send_sem=pre_s.at[to, u], recv_sem=pre_r.at[frm, u],
            device_id=(g * G + to, e), device_id_type=MESH,
        )

    def chain_copy(u):
        return pltpu.make_async_remote_copy(
            src_ref=chain_out.at[u], dst_ref=chain_in.at[u],
            send_sem=ch_s.at[u], recv_sem=ch_r.at[u],
            device_id=((s + G) % n, e), device_id_type=MESH,
        )

    fetch_k.wait()
    fetch_v.wait()
    for h in range(heads):
        intra[h] = jnp.broadcast_to(key_w[:, h : h + 1], (T, HD))
    for u in range(SUB):
        for i in list(range(1, G)) + [0]:
            to = member(i)
            for r in range(hb):
                h = to * HS + u * hb + r
                lanes = pl.ds(pl.multiple_of(h * HD, HD), HD)
                high, low = split_high_low(k_ref[:, lanes].astype(F32) * intra[h])
                value = v_ref[:, lanes]
                memory = lax.dot_general(
                    jnp.concatenate([high, low], axis=0),
                    jnp.concatenate([value, value], axis=0),
                    (((0,), (0,)), ((), ())),
                    preferred_element_type=F32,
                )
                if i == 0:
                    mem_in[c, u, r] = memory
                else:
                    mem_own[to, u, r] = memory
            if u == 0 and i == 1:
                beside = (g + NG - 1) // NG + (2 * NG - 2 - g) // NG
                pl.semaphore_wait(barrier, (G - 1) + (nh - 1) + beside)
                for o in range(1, G):
                    dec_copy(member(o), c).start()
            if i > 0:
                mem_copy(to, c, u).start()
    dec_in[c] = dec_own[c]
    for copy in w_copies:
        copy.start()

    for copy in (fetch_q, fetch_gain, fetch_ids, fetch_tab):
        copy.wait()
    for h in range(heads):
        lanes = slice(h * HD, (h + 1) * HD)
        scores = lax.dot_general(
            q_ref[:, lanes], k_ref[:, lanes], (((1,), (1,)), ((), ())),
            preferred_element_type=F32,
        )
        diffs = jnp.where(lower, cum[:, h : h + 1] - cum_row[h : h + 1, :], 0.0)
        weights = (jnp.where(lower, jnp.exp(diffs), 0.0) * scores).astype(BF16)
        intra[h] = jnp.dot(weights, v_ref[:, lanes], preferred_element_type=F32)
        ecb[h] = jnp.broadcast_to(grow[:, h : h + 1], (T, HD))
    nsteer = tab_ref.shape[0]
    ids = jnp.broadcast_to(ids_ref[...], (nsteer, T))
    onehot = jnp.where(ids == lax.broadcasted_iota(jnp.int32, (nsteer, T), 0), 1.0, 0.0).astype(BF16)
    acc[...] = jnp.zeros_like(acc)
    acc[:, pl.ds(pl.multiple_of(e * CW, CW), CW)] = lax.dot_general(
        onehot, tab_ref[...], (((0,), (0,)), ((), ())), preferred_element_type=F32
    )

    for o in range(1, G):
        dec_copy(c, member(o)).wait_recv()
    for u in range(SUB):
        for o in range(1, G):
            mem_copy(c, member(o), u).wait_recv()

        @pl.when(g > 0)
        def _():
            chain_copy(u).wait_recv()

        @pl.when(g == 0)
        def _():
            chain_in[u] = jnp.zeros(chain_in.shape[1:], F32)

        for r in range(hb):
            state = chain_in[u, r]
            row = u * hb + r
            for j in range(G):
                pre_out[j, u, r] = state
                state = state * dec_in[j, row : row + 1, :] + mem_in[j, u, r]
            chain_out[u, r] = state

        @pl.when(g < NG - 1)
        def _():
            chain_copy(u).start()

        for o in range(1, G):
            pre_copy(member(o), c, u).start()
        pre_in[c, u] = pre_out[c, u]

    pair = 2 if SUB % 2 == 0 else 1

    def normed_chunk(j, p):
        parts = []
        for d in range(pair):
            u = p * pair + d
            for r in range(hb):
                h = j * HS + u * hb + r
                lanes = pl.ds(pl.multiple_of(h * HD, HD), HD)
                high, low = split_high_low(pre_in[j, u, r])
                query = q_ref[:, lanes]
                carried = jnp.dot(
                    jnp.concatenate([query, query], axis=1),
                    jnp.concatenate([high, low], axis=0),
                    preferred_element_type=F32,
                )
                attended = intra[h] + ecb[h] * carried
                mean_sq = jnp.mean(attended * attended, axis=1, keepdims=True)
                normed = attended * lax.rsqrt(mean_sq + 1e-6) * gain_ref[:, lanes]
                parts.append(normed.astype(BF16))
        return parts[0] if len(parts) == 1 else jnp.concatenate(parts, axis=1)

    def w_rows(j, p):
        depth = pair * hb * HD
        return pl.ds(pl.multiple_of(j * HS * HD + p * depth, HD), depth)

    for copy in w_copies:
        copy.wait()

    def step(i, carry):
        p, o = i // G, i % G
        j = member(o)

        @pl.when(o > 0)
        def _():
            for d in range(pair):
                pre_copy(c, j, p * pair + d).wait_recv()

        chunk = normed_chunk(j, p)
        for t in range(width // TW):
            at = slice(t * TW, (t + 1) * TW)
            acc[:, at] += jnp.dot(chunk, w_ref[w_rows(j, p), at], preferred_element_type=F32)
        return carry

    lax.fori_loop(0, G * (SUB // pair) - 1, step, 0)

    last = member(G - 1)
    final = SUB // pair - 1
    for d in range(pair):
        pre_copy(c, last, final * pair + d).wait_recv()
    chunk = normed_chunk(last, final)
    rows_last = w_rows(last, final)

    def x_copy(o, t):
        return pltpu.make_async_remote_copy(
            src_ref=xout.at[o - 1, t], dst_ref=xin.at[o - 1, t],
            send_sem=x_s.at[o - 1, t], recv_sem=x_r.at[o - 1, t],
            device_id=(s, (e + o) % nh), device_id_type=MESH,
        )

    for o in range(1, nh):
        to = (e + o) % nh
        for t in range(nt):
            at = pl.ds(pl.multiple_of(to * CW + t * TW, TW), TW)
            xout[o - 1, t] = acc[:, at] + jnp.dot(
                chunk, w_ref[rows_last, at], preferred_element_type=F32
            )
            x_copy(o, t).start()
    for t in range(nt):
        at = pl.ds(pl.multiple_of(e * CW + t * TW, TW), TW)
        acc[:, at] += jnp.dot(chunk, w_ref[rows_last, at], preferred_element_type=F32)
    for t in range(nt):
        at = pl.ds(pl.multiple_of(e * CW + t * TW, TW), TW)
        whole = acc[:, at]
        for o in range(1, nh):
            x_copy(o, t).wait_recv()
            whole = whole + xin[o - 1, t]
        out_ref[:, t * TW : (t + 1) * TW] = whole.astype(BF16)

    for o in range(1, G):
        dec_copy(member(o), c).wait_send()
        for u in range(SUB):
            mem_copy(member(o), c, u).wait_send()
            pre_copy(member(o), c, u).wait_send()
    for o in range(1, nh):
        for t in range(nt):
            x_copy(o, t).wait_send()

    @pl.when(g < NG - 1)
    def _():
        for u in range(SUB):
            chain_copy(u).wait_send()


def solution(mesh):
    n, nh = mesh.shape["seq"], mesh.shape["head"]

    def shards(queries, keys, values, log_decay, norm_gain, out_weight, steer_ids, steer_table):
        T, features = queries.shape
        heads = log_decay.shape[1]
        HD = features // heads
        width = out_weight.shape[1]
        CW = width // nh
        G = 4
        HS = heads // G
        hb = 1
        SUB = HS // hb
        nt = max(1, CW // 512)
        TW = CW // nt
        pad = (HS + 7) // 8 * 8
        DMA = pltpu.SemaphoreType.DMA
        return pl.pallas_call(
            functools.partial(kernel, n, nh, G, SUB, hb, nt),
            out_shape=jax.ShapeDtypeStruct((T, CW), BF16),
            in_specs=[pl.BlockSpec(memory_space=pltpu.HBM)] * 8,
            out_specs=pl.BlockSpec(memory_space=pltpu.VMEM),
            scratch_shapes=[
                pltpu.VMEM((T, features), BF16),
                pltpu.VMEM((T, features), BF16),
                pltpu.VMEM((T, features), BF16),
                pltpu.VMEM((heads, T), F32),
                pltpu.VMEM((1, features), F32),
                pltpu.VMEM((1, T), jnp.int32),
                pltpu.VMEM(steer_table.shape, BF16),
                DMA((7,)),
                pltpu.VMEM((features, width), BF16),
                pltpu.VMEM((G, SUB, hb, HD, HD), F32),
                pltpu.VMEM((G, pad, HD), F32),
                pltpu.VMEM((G, SUB, hb, HD, HD), F32),
                pltpu.VMEM((G, pad, HD), F32),
                pltpu.VMEM((SUB, hb, HD, HD), F32),
                pltpu.VMEM((SUB, hb, HD, HD), F32),
                pltpu.VMEM((G, SUB, hb, HD, HD), F32),
                pltpu.VMEM((G, SUB, hb, HD, HD), F32),
                pltpu.VMEM((heads, T, HD), F32),
                pltpu.VMEM((heads, T, HD), F32),
                pltpu.VMEM((T, width), F32),
                pltpu.VMEM((nh - 1, nt, T, TW), F32),
                pltpu.VMEM((nh - 1, nt, T, TW), F32),
                DMA((W_COPIES,)),
                DMA((G, SUB)), DMA((G, SUB)),
                DMA((G,)), DMA((G,)),
                DMA((SUB,)), DMA((SUB,)),
                DMA((G, SUB)), DMA((G, SUB)),
                DMA((nh - 1, nt)), DMA((nh - 1, nt)),
            ],
            compiler_params=pltpu.CompilerParams(
                collective_id=0, has_side_effects=True, vmem_limit_bytes=60 * 1024 * 1024
            ),
            cost_estimate=pl.CostEstimate(
                flops=2 * T * features * width,
                bytes_accessed=2 * features * width,
                transcendentals=T * T * heads,
            ),
        )(
            queries, keys, values, log_decay.T, norm_gain.reshape(1, features), out_weight,
            steer_ids.reshape(1, T), steer_table,
        )

    in_specs = (
        P("seq", "head"), P("seq", "head"), P("seq", "head"), P("seq", "head"),
        P("head"), P("head", None), P("seq"), P(None, "head"),
    )
    return jax.shard_map(
        shards, mesh=mesh, in_specs=in_specs, out_specs=P("seq", "head"), check_vma=False
    )
```

```python
import functools

import jax
import jax.numpy as jnp
from jax import lax
from jax.experimental import pallas as pl
from jax.experimental.pallas import tpu as pltpu
from jax.sharding import PartitionSpec as P

MESH = pl.DeviceIdType.MESH
F32 = jnp.float32
BF16 = jnp.bfloat16
W_COPIES = 8


def split_high_low(x):
    high = x.astype(BF16)
    return high, (x - high.astype(F32)).astype(BF16)


def kernel(
    n, nh, G, SUB, hb, nt,
    q_hbm, k_hbm, v_hbm, ld_hbm, gain_hbm, w_hbm, ids_hbm, tab_hbm,
    out_ref,
    q_ref, k_ref, v_ref, ld_ref, gain_ref, ids_ref, tab_ref, in_sem,
    w_ref, mem_own, dec_own, mem_in, dec_in, chain_out, chain_in, pre_out, pre_in,
    intra, ecb, acc, xout, xin, late_w_out, late_w_in, late_out, late_in,
    w_sem, mem_s, mem_r, dec_s, dec_r, ch_s, ch_r, pre_s, pre_r, x_s, x_r, lw_s, lw_r, la_s, la_r,
):
    T, features = q_hbm.shape
    HD = 128
    heads = features // HD
    HS = heads // G
    NG = n // G
    width = w_hbm.shape[1]
    CW = width // nh
    TW = CW // nt
    s = lax.axis_index("seq")
    e = lax.axis_index("head")
    g = s // G
    c = s % G

    def member(i):
        o, bit, rank = (G - i) % G, 1, 0
        while bit < G:
            rank = rank + (c // bit + o // bit) % 2 * bit
            bit *= 2
        return rank

    fetch_ld, fetch_k, fetch_v, fetch_q, fetch_gain, fetch_ids, fetch_tab = [
        pltpu.make_async_copy(src, dst, in_sem.at[i])
        for i, (src, dst) in enumerate(
            [
                (ld_hbm, ld_ref), (k_hbm, k_ref), (v_hbm, v_ref), (q_hbm, q_ref),
                (gain_hbm, gain_ref), (ids_hbm, ids_ref), (tab_hbm, tab_ref),
            ]
        )
    ]
    for copy in (fetch_ld, fetch_k, fetch_v, fetch_q, fetch_gain, fetch_ids, fetch_tab):
        copy.start()

    barrier = pltpu.get_barrier_semaphore()
    for o in range(1, G):
        pl.semaphore_signal(barrier, 1, device_id=(g * G + member(o), e), device_id_type=MESH)
    for o in range(1, nh):
        pl.semaphore_signal(barrier, 1, device_id=(s, (e + o) % nh), device_id_type=MESH)

    @pl.when(g > 0)
    def _():
        pl.semaphore_signal(barrier, 1, device_id=(s - G, e), device_id_type=MESH)

    @pl.when(g < NG - 1)
    def _():
        pl.semaphore_signal(barrier, 1, device_id=(s + G, e), device_id_type=MESH)

    wr = features // W_COPIES
    w_copies = [
        pltpu.make_async_copy(
            w_hbm.at[pl.ds(i * wr, wr)], w_ref.at[pl.ds(i * wr, wr)], w_sem.at[i]
        )
        for i in range(W_COPIES)
    ]

    fetch_ld.wait()
    ld = ld_ref[...]
    rows = lax.broadcasted_iota(jnp.int32, (T, T), 0)
    cols = lax.broadcasted_iota(jnp.int32, (T, T), 1)
    lower = cols <= rows
    tril = jnp.where(lower, 1.0, 0.0).astype(F32)
    cum = lax.dot_general(
        tril, ld, (((1,), (1,)), ((), ())),
        precision=lax.Precision.HIGHEST, preferred_element_type=F32,
    )
    cum_row = lax.dot_general(
        ld, tril, (((1,), (1,)), ((), ())),
        precision=lax.Precision.HIGHEST, preferred_element_type=F32,
    )
    total_row = cum[T - 1 : T, :]
    key_w = jnp.exp(total_row - cum)
    grow = jnp.exp(cum)
    block_decay = jnp.broadcast_to(jnp.exp(cum_row[:, T - 1 : T]), (heads, HD))
    pad = dec_own.shape[1]
    for j in range(G):
        part = block_decay[j * HS : (j + 1) * HS, :]
        if pad > HS:
            part = jnp.concatenate([part, jnp.zeros((pad - HS, HD), F32)], axis=0)
        dec_own[j] = part

    def dec_copy(to, frm):
        return pltpu.make_async_remote_copy(
            src_ref=dec_own.at[to], dst_ref=dec_in.at[frm],
            send_sem=dec_s.at[to], recv_sem=dec_r.at[frm],
            device_id=(g * G + to, e), device_id_type=MESH,
        )

    def mem_copy(to, frm, u):
        return pltpu.make_async_remote_copy(
            src_ref=mem_own.at[to, u], dst_ref=mem_in.at[frm, u],
            send_sem=mem_s.at[to, u], recv_sem=mem_r.at[frm, u],
            device_id=(g * G + to, e), device_id_type=MESH,
        )

    def pre_copy(to, frm, u):
        return pltpu.make_async_remote_copy(
            src_ref=pre_out.at[to, u], dst_ref=pre_in.at[frm, u],
            send_sem=pre_s.at[to, u], recv_sem=pre_r.at[frm, u],
            device_id=(g * G + to, e), device_id_type=MESH,
        )

    def chain_copy(u):
        return pltpu.make_async_remote_copy(
            src_ref=chain_out.at[u], dst_ref=chain_in.at[u],
            send_sem=ch_s.at[u], recv_sem=ch_r.at[u],
            device_id=((s + G) % n, e), device_id_type=MESH,
        )

    fetch_k.wait()
    fetch_v.wait()
    for h in range(heads):
        intra[h] = jnp.broadcast_to(key_w[:, h : h + 1], (T, HD))
    for u in range(SUB):
        for i in list(range(1, G)) + [0]:
            to = member(i)
            for r in range(hb):
                h = to * HS + u * hb + r
                lanes = pl.ds(pl.multiple_of(h * HD, HD), HD)
                high, low = split_high_low(k_ref[:, lanes].astype(F32) * intra[h])
                value = v_ref[:, lanes]
                memory = lax.dot_general(
                    jnp.concatenate([high, low], axis=0),
                    jnp.concatenate([value, value], axis=0),
                    (((0,), (0,)), ((), ())),
                    preferred_element_type=F32,
                )
                if i == 0:
                    mem_in[c, u, r] = memory
                else:
                    mem_own[to, u, r] = memory
            if u == 0 and i == 1:
                beside = (g + NG - 1) // NG + (2 * NG - 2 - g) // NG
                pl.semaphore_wait(barrier, (G - 1) + (nh - 1) + beside)
                for o in range(1, G):
                    dec_copy(member(o), c).start()
            if i > 0:
                mem_copy(to, c, u).start()
    dec_in[c] = dec_own[c]
    for copy in w_copies:
        copy.start()

    for copy in (fetch_q, fetch_gain, fetch_ids, fetch_tab):
        copy.wait()
    for h in range(heads):
        lanes = slice(h * HD, (h + 1) * HD)
        scores = lax.dot_general(
            q_ref[:, lanes], k_ref[:, lanes], (((1,), (1,)), ((), ())),
            preferred_element_type=F32,
        )
        diffs = jnp.where(lower, cum[:, h : h + 1] - cum_row[h : h + 1, :], 0.0)
        weights = (jnp.where(lower, jnp.exp(diffs), 0.0) * scores).astype(BF16)
        intra[h] = jnp.dot(weights, v_ref[:, lanes], preferred_element_type=F32)
        ecb[h] = jnp.broadcast_to(grow[:, h : h + 1], (T, HD))
    nsteer = tab_ref.shape[0]
    ids = jnp.broadcast_to(ids_ref[...], (nsteer, T))
    onehot = jnp.where(ids == lax.broadcasted_iota(jnp.int32, (nsteer, T), 0), 1.0, 0.0).astype(BF16)
    acc[...] = jnp.zeros_like(acc)
    acc[:, pl.ds(pl.multiple_of(e * CW, CW), CW)] = lax.dot_general(
        onehot, tab_ref[...], (((0,), (0,)), ((), ())), preferred_element_type=F32
    )

    for o in range(1, G):
        dec_copy(c, member(o)).wait_recv()
    for u in range(SUB):
        for o in range(1, G):
            mem_copy(c, member(o), u).wait_recv()

        @pl.when(g > 0)
        def _():
            chain_copy(u).wait_recv()

        @pl.when(g == 0)
        def _():
            chain_in[u] = jnp.zeros(chain_in.shape[1:], F32)

        for r in range(hb):
            state = chain_in[u, r]
            row = u * hb + r
            for j in range(G):
                pre_out[j, u, r] = state
                state = state * dec_in[j, row : row + 1, :] + mem_in[j, u, r]
            chain_out[u, r] = state

        @pl.when(g < NG - 1)
        def _():
            chain_copy(u).start()

        for o in range(1, G):
            pre_copy(member(o), c, u).start()
        pre_in[c, u] = pre_out[c, u]

    pair = 2 if SUB % 2 == 0 else 1

    def normed_chunk(j, p):
        parts = []
        for d in range(pair):
            u = p * pair + d
            for r in range(hb):
                h = j * HS + u * hb + r
                lanes = pl.ds(pl.multiple_of(h * HD, HD), HD)
                high, low = split_high_low(pre_in[j, u, r])
                query = q_ref[:, lanes]
                carried = jnp.dot(
                    jnp.concatenate([query, query], axis=1),
                    jnp.concatenate([high, low], axis=0),
                    preferred_element_type=F32,
                )
                attended = intra[h] + ecb[h] * carried
                mean_sq = jnp.mean(attended * attended, axis=1, keepdims=True)
                normed = attended * lax.rsqrt(mean_sq + 1e-6) * gain_ref[:, lanes]
                parts.append(normed.astype(BF16))
        return parts[0] if len(parts) == 1 else jnp.concatenate(parts, axis=1)

    def w_rows(j, p):
        depth = pair * hb * HD
        return pl.ds(pl.multiple_of(j * HS * HD + p * depth, HD), depth)

    for copy in w_copies:
        copy.wait()

    def step(i, carry):
        p, o = i // G, i % G
        j = member(o)

        @pl.when(o > 0)
        def _():
            for d in range(pair):
                pre_copy(c, j, p * pair + d).wait_recv()

        chunk = normed_chunk(j, p)
        for t in range(width // TW):
            at = slice(t * TW, (t + 1) * TW)
            acc[:, at] += jnp.dot(chunk, w_ref[w_rows(j, p), at], preferred_element_type=F32)
        return carry

    last = member(G - 1)
    final = SUB // pair - 1
    rows_last = w_rows(last, final)

    def late_w_copy(o):
        return pltpu.make_async_remote_copy(
            src_ref=late_w_out.at[o - 1], dst_ref=late_w_in.at[o - 1],
            send_sem=lw_s.at[o - 1], recv_sem=lw_r.at[o - 1],
            device_id=(s, (e + o) % nh), device_id_type=MESH,
        )

    def late_copy(o):
        return pltpu.make_async_remote_copy(
            src_ref=late_out, dst_ref=late_in.at[o - 1],
            send_sem=la_s.at[o - 1], recv_sem=la_r.at[o - 1],
            device_id=(s, (e + o) % nh), device_id_type=MESH,
        )

    def x_copy(o, t):
        return pltpu.make_async_remote_copy(
            src_ref=xout.at[o - 1, t], dst_ref=xin.at[o - 1, t],
            send_sem=x_s.at[o - 1, t], recv_sem=x_r.at[o - 1, t],
            device_id=(s, (e + o) % nh), device_id_type=MESH,
        )

    def columns(group, t):
        return pl.ds(pl.multiple_of(group * CW + t * TW, TW), TW)

    for o in range(1, nh):
        to = (e + o) % nh
        for t in range(nt):
            late_w_out[o - 1, :, t * TW : (t + 1) * TW] = w_ref[rows_last, columns(to, t)].astype(F32)
        late_w_copy(o).start()

    lax.fori_loop(0, G * (SUB // pair) - 1, step, 0)

    for o in range(1, nh):
        to = (e + o) % nh
        for t in range(nt):
            xout[o - 1, t] = acc[:, columns(to, t)]
            x_copy(o, t).start()

    for d in range(pair):
        pre_copy(c, last, final * pair + d).wait_recv()
    chunk = normed_chunk(last, final)
    late_out[...] = chunk.astype(F32)
    for o in range(1, nh):
        late_copy(o).start()
    for t in range(nt):
        at = columns(e, t)
        acc[:, at] += jnp.dot(chunk, w_ref[rows_last, at], preferred_element_type=F32)
    for o in range(1, nh):
        late_w_copy(o).wait_recv()
        for t in range(nt):
            x_copy(o, t).wait_recv()
    for o in range(1, nh):
        late_copy(o).wait_recv()
    for t in range(nt):
        at = slice(t * TW, (t + 1) * TW)
        whole = acc[:, columns(e, t)]
        for o in range(1, nh):
            whole = whole + xin[o - 1, t] + jnp.dot(
                late_in[o - 1].astype(BF16), late_w_in[o - 1, :, at].astype(BF16),
                preferred_element_type=F32,
            )
        out_ref[:, at] = whole.astype(BF16)

    for o in range(1, G):
        dec_copy(member(o), c).wait_send()
        for u in range(SUB):
            mem_copy(member(o), c, u).wait_send()
            pre_copy(member(o), c, u).wait_send()
    for o in range(1, nh):
        for t in range(nt):
            x_copy(o, t).wait_send()
        late_w_copy(o).wait_send()
        late_copy(o).wait_send()

    @pl.when(g < NG - 1)
    def _():
        for u in range(SUB):
            chain_copy(u).wait_send()


def solution(mesh):
    n, nh = mesh.shape["seq"], mesh.shape["head"]

    def shards(queries, keys, values, log_decay, norm_gain, out_weight, steer_ids, steer_table):
        T, features = queries.shape
        heads = log_decay.shape[1]
        HD = features // heads
        width = out_weight.shape[1]
        CW = width // nh
        G = 4
        HS = heads // G
        hb = 1
        SUB = HS // hb
        nt = max(1, CW // 512)
        TW = CW // nt
        pad = (HS + 7) // 8 * 8
        late = (2 if SUB % 2 == 0 else 1) * hb * HD
        DMA = pltpu.SemaphoreType.DMA
        return pl.pallas_call(
            functools.partial(kernel, n, nh, G, SUB, hb, nt),
            out_shape=jax.ShapeDtypeStruct((T, CW), BF16),
            in_specs=[pl.BlockSpec(memory_space=pltpu.HBM)] * 8,
            out_specs=pl.BlockSpec(memory_space=pltpu.VMEM),
            scratch_shapes=[
                pltpu.VMEM((T, features), BF16),
                pltpu.VMEM((T, features), BF16),
                pltpu.VMEM((T, features), BF16),
                pltpu.VMEM((heads, T), F32),
                pltpu.VMEM((1, features), F32),
                pltpu.VMEM((1, T), jnp.int32),
                pltpu.VMEM(steer_table.shape, BF16),
                DMA((7,)),
                pltpu.VMEM((features, width), BF16),
                pltpu.VMEM((G, SUB, hb, HD, HD), F32),
                pltpu.VMEM((G, pad, HD), F32),
                pltpu.VMEM((G, SUB, hb, HD, HD), F32),
                pltpu.VMEM((G, pad, HD), F32),
                pltpu.VMEM((SUB, hb, HD, HD), F32),
                pltpu.VMEM((SUB, hb, HD, HD), F32),
                pltpu.VMEM((G, SUB, hb, HD, HD), F32),
                pltpu.VMEM((G, SUB, hb, HD, HD), F32),
                pltpu.VMEM((heads, T, HD), F32),
                pltpu.VMEM((heads, T, HD), F32),
                pltpu.VMEM((T, width), F32),
                pltpu.VMEM((nh - 1, nt, T, TW), F32),
                pltpu.VMEM((nh - 1, nt, T, TW), F32),
                pltpu.VMEM((nh - 1, late, CW), F32),
                pltpu.VMEM((nh - 1, late, CW), F32),
                pltpu.VMEM((T, late), F32),
                pltpu.VMEM((nh - 1, T, late), F32),
                DMA((W_COPIES,)),
                DMA((G, SUB)), DMA((G, SUB)),
                DMA((G,)), DMA((G,)),
                DMA((SUB,)), DMA((SUB,)),
                DMA((G, SUB)), DMA((G, SUB)),
                DMA((nh - 1, nt)), DMA((nh - 1, nt)),
                DMA((nh - 1,)), DMA((nh - 1,)),
                DMA((nh - 1,)), DMA((nh - 1,)),
            ],
            compiler_params=pltpu.CompilerParams(
                collective_id=0, has_side_effects=True, vmem_limit_bytes=60 * 1024 * 1024
            ),
            cost_estimate=pl.CostEstimate(
                flops=2 * T * features * width,
                bytes_accessed=2 * features * width,
                transcendentals=T * T * heads,
            ),
        )(
            queries, keys, values, log_decay.T, norm_gain.reshape(1, features), out_weight,
            steer_ids.reshape(1, T), steer_table,
        )

    in_specs = (
        P("seq", "head"), P("seq", "head"), P("seq", "head"), P("seq", "head"),
        P("head"), P("head", None), P("seq"), P(None, "head"),
    )
    return jax.shard_map(
        shards, mesh=mesh, in_specs=in_specs, out_specs=P("seq", "head"), check_vma=False
    )
```

```python
import functools

import jax
import jax.numpy as jnp
from jax import lax
from jax.experimental import pallas as pl
from jax.experimental.pallas import tpu as pltpu
from jax.sharding import PartitionSpec as P

MESH = pl.DeviceIdType.MESH
F32 = jnp.float32
BF16 = jnp.bfloat16
W_COPIES = 8


def split_high_low(x):
    high = x.astype(BF16)
    return high, (x - high.astype(F32)).astype(BF16)


def kernel(
    n, nh, G, SUB, hb, nt,
    q_hbm, k_hbm, v_hbm, ld_hbm, gain_hbm, w_hbm, ids_hbm, tab_hbm,
    out_ref,
    q_ref, k_ref, v_ref, ld_ref, gain_ref, ids_ref, tab_ref, in_sem,
    w_ref, mem_own, dec_own, mem_in, dec_in, chain_out, chain_in, pre_out, pre_in,
    intra, ecb, acc, xout, xin,
    w_sem, mem_s, mem_r, dec_s, dec_r, ch_s, ch_r, pre_s, pre_r, x_s, x_r,
):
    T, features = q_hbm.shape
    HD = 128
    heads = features // HD
    HS = heads // G
    NG = n // G
    width = w_hbm.shape[1]
    CW = width // nh
    TW = CW // nt
    s = lax.axis_index("seq")
    e = lax.axis_index("head")
    g = s // G
    c = s % G

    def member(i):
        o, bit, rank = (G - i) % G, 1, 0
        while bit < G:
            rank = rank + (c // bit + o // bit) % 2 * bit
            bit *= 2
        return rank

    fetch_ld, fetch_k, fetch_v, fetch_q, fetch_gain, fetch_ids, fetch_tab = [
        pltpu.make_async_copy(src, dst, in_sem.at[i])
        for i, (src, dst) in enumerate(
            [
                (ld_hbm, ld_ref), (k_hbm, k_ref), (v_hbm, v_ref), (q_hbm, q_ref),
                (gain_hbm, gain_ref), (ids_hbm, ids_ref), (tab_hbm, tab_ref),
            ]
        )
    ]
    for copy in (fetch_ld, fetch_k, fetch_v, fetch_q, fetch_gain, fetch_ids, fetch_tab):
        copy.start()

    barrier = pltpu.get_barrier_semaphore()
    for o in range(1, G):
        pl.semaphore_signal(barrier, 1, device_id=(g * G + member(o), e), device_id_type=MESH)
    for o in range(1, nh):
        pl.semaphore_signal(barrier, 1, device_id=(s, (e + o) % nh), device_id_type=MESH)

    @pl.when(g > 0)
    def _():
        pl.semaphore_signal(barrier, 1, device_id=(s - G, e), device_id_type=MESH)

    @pl.when(g < NG - 1)
    def _():
        pl.semaphore_signal(barrier, 1, device_id=(s + G, e), device_id_type=MESH)

    wr = features // W_COPIES
    w_copies = [
        pltpu.make_async_copy(
            w_hbm.at[pl.ds(i * wr, wr)], w_ref.at[pl.ds(i * wr, wr)], w_sem.at[i]
        )
        for i in range(W_COPIES)
    ]

    fetch_ld.wait()
    ld = ld_ref[...]
    rows = lax.broadcasted_iota(jnp.int32, (T, T), 0)
    cols = lax.broadcasted_iota(jnp.int32, (T, T), 1)
    lower = cols <= rows
    tril = jnp.where(lower, 1.0, 0.0).astype(F32)
    cum = lax.dot_general(
        tril, ld, (((1,), (1,)), ((), ())),
        precision=lax.Precision.HIGHEST, preferred_element_type=F32,
    )
    cum_row = lax.dot_general(
        ld, tril, (((1,), (1,)), ((), ())),
        precision=lax.Precision.HIGHEST, preferred_element_type=F32,
    )
    total_row = cum[T - 1 : T, :]
    key_w = jnp.exp(total_row - cum)
    grow = jnp.exp(cum)
    block_decay = jnp.broadcast_to(jnp.exp(cum_row[:, T - 1 : T]), (heads, HD))
    pad = dec_own.shape[1]
    for j in range(G):
        part = block_decay[j * HS : (j + 1) * HS, :]
        if pad > HS:
            part = jnp.concatenate([part, jnp.zeros((pad - HS, HD), F32)], axis=0)
        dec_own[j] = part

    def dec_copy(to, frm):
        return pltpu.make_async_remote_copy(
            src_ref=dec_own.at[to], dst_ref=dec_in.at[frm],
            send_sem=dec_s.at[to], recv_sem=dec_r.at[frm],
            device_id=(g * G + to, e), device_id_type=MESH,
        )

    def mem_copy(to, frm, u):
        return pltpu.make_async_remote_copy(
            src_ref=mem_own.at[to, u], dst_ref=mem_in.at[frm, u],
            send_sem=mem_s.at[to, u], recv_sem=mem_r.at[frm, u],
            device_id=(g * G + to, e), device_id_type=MESH,
        )

    def pre_copy(to, frm, u):
        return pltpu.make_async_remote_copy(
            src_ref=pre_out.at[to, u], dst_ref=pre_in.at[frm, u],
            send_sem=pre_s.at[to, u], recv_sem=pre_r.at[frm, u],
            device_id=(g * G + to, e), device_id_type=MESH,
        )

    def chain_copy(u):
        return pltpu.make_async_remote_copy(
            src_ref=chain_out.at[u], dst_ref=chain_in.at[u],
            send_sem=ch_s.at[u], recv_sem=ch_r.at[u],
            device_id=((s + G) % n, e), device_id_type=MESH,
        )

    fetch_k.wait()
    fetch_v.wait()
    for h in range(heads):
        intra[h] = jnp.broadcast_to(key_w[:, h : h + 1], (T, HD))
    for u in range(SUB):
        for i in list(range(1, G)) + [0]:
            to = member(i)
            for r in range(hb):
                h = to * HS + u * hb + r
                lanes = pl.ds(pl.multiple_of(h * HD, HD), HD)
                high, low = split_high_low(k_ref[:, lanes].astype(F32) * intra[h])
                value = v_ref[:, lanes]
                memory = lax.dot_general(
                    jnp.concatenate([high, low], axis=0),
                    jnp.concatenate([value, value], axis=0),
                    (((0,), (0,)), ((), ())),
                    preferred_element_type=F32,
                )
                if i == 0:
                    mem_in[c, u, r] = memory
                else:
                    mem_own[to, u, r] = memory
            if u == 0 and i == 1:
                beside = (g + NG - 1) // NG + (2 * NG - 2 - g) // NG
                pl.semaphore_wait(barrier, (G - 1) + (nh - 1) + beside)
                for o in range(1, G):
                    dec_copy(member(o), c).start()
            if i > 0 and u < 2:
                mem_copy(to, c, u).start()
    dec_in[c] = dec_own[c]
    for copy in w_copies:
        copy.start()

    for copy in (fetch_q, fetch_gain, fetch_ids, fetch_tab):
        copy.wait()
    for h in range(heads):
        if SUB > 2 and h % (heads // (SUB - 2)) == heads // (SUB - 2) - 1:
            u = 2 + h // (heads // (SUB - 2))
            for o in range(1, G):
                mem_copy(member(o), c, u - 2).wait_send()
            for o in range(1, G):
                mem_copy(member(o), c, u).start()
        lanes = slice(h * HD, (h + 1) * HD)
        scores = lax.dot_general(
            q_ref[:, lanes], k_ref[:, lanes], (((1,), (1,)), ((), ())),
            preferred_element_type=F32,
        )
        diffs = jnp.where(lower, cum[:, h : h + 1] - cum_row[h : h + 1, :], 0.0)
        weights = (jnp.where(lower, jnp.exp(diffs), 0.0) * scores).astype(BF16)
        intra[h] = jnp.dot(weights, v_ref[:, lanes], preferred_element_type=F32)
        ecb[h] = jnp.broadcast_to(grow[:, h : h + 1], (T, HD))
    nsteer = tab_ref.shape[0]
    ids = jnp.broadcast_to(ids_ref[...], (nsteer, T))
    onehot = jnp.where(ids == lax.broadcasted_iota(jnp.int32, (nsteer, T), 0), 1.0, 0.0).astype(BF16)
    acc[...] = jnp.zeros_like(acc)
    acc[:, pl.ds(pl.multiple_of(e * CW, CW), CW)] = lax.dot_general(
        onehot, tab_ref[...], (((0,), (0,)), ((), ())), preferred_element_type=F32
    )

    for o in range(1, G):
        dec_copy(c, member(o)).wait_recv()
    for u in range(SUB):
        for o in range(1, G):
            mem_copy(c, member(o), u).wait_recv()

        @pl.when(g > 0)
        def _():
            chain_copy(u).wait_recv()

        @pl.when(g == 0)
        def _():
            chain_in[u] = jnp.zeros(chain_in.shape[1:], F32)

        for r in range(hb):
            state = chain_in[u, r]
            row = u * hb + r
            for j in range(G):
                pre_out[j, u, r] = state
                state = state * dec_in[j, row : row + 1, :] + mem_in[j, u, r]
            chain_out[u, r] = state

        @pl.when(g < NG - 1)
        def _():
            chain_copy(u).start()

        for o in range(1, G):
            pre_copy(member(o), c, u).start()
        pre_in[c, u] = pre_out[c, u]

    pair = 2 if SUB % 2 == 0 else 1

    def normed_chunk(j, p):
        parts = []
        for d in range(pair):
            u = p * pair + d
            for r in range(hb):
                h = j * HS + u * hb + r
                lanes = pl.ds(pl.multiple_of(h * HD, HD), HD)
                high, low = split_high_low(pre_in[j, u, r])
                query = q_ref[:, lanes]
                carried = jnp.dot(
                    jnp.concatenate([query, query], axis=1),
                    jnp.concatenate([high, low], axis=0),
                    preferred_element_type=F32,
                )
                attended = intra[h] + ecb[h] * carried
                mean_sq = jnp.mean(attended * attended, axis=1, keepdims=True)
                normed = attended * lax.rsqrt(mean_sq + 1e-6) * gain_ref[:, lanes]
                parts.append(normed.astype(BF16))
        return parts[0] if len(parts) == 1 else jnp.concatenate(parts, axis=1)

    def w_rows(j, p):
        depth = pair * hb * HD
        return pl.ds(pl.multiple_of(j * HS * HD + p * depth, HD), depth)

    for copy in w_copies:
        copy.wait()

    def step(i, carry):
        p, o = i // G, i % G
        j = member(o)

        @pl.when(o > 0)
        def _():
            for d in range(pair):
                pre_copy(c, j, p * pair + d).wait_recv()

        chunk = normed_chunk(j, p)
        for t in range(width // TW):
            at = slice(t * TW, (t + 1) * TW)
            acc[:, at] += jnp.dot(chunk, w_ref[w_rows(j, p), at], preferred_element_type=F32)
        return carry

    lax.fori_loop(0, G * (SUB // pair) - 1, step, 0)

    last = member(G - 1)
    final = SUB // pair - 1
    for d in range(pair):
        pre_copy(c, last, final * pair + d).wait_recv()
    chunk = normed_chunk(last, final)
    rows_last = w_rows(last, final)

    def x_copy(o, t):
        return pltpu.make_async_remote_copy(
            src_ref=xout.at[o - 1, t], dst_ref=xin.at[o - 1, t],
            send_sem=x_s.at[o - 1, t], recv_sem=x_r.at[o - 1, t],
            device_id=(s, (e + o) % nh), device_id_type=MESH,
        )

    for o in range(1, nh):
        to = (e + o) % nh
        for t in range(nt):
            at = pl.ds(pl.multiple_of(to * CW + t * TW, TW), TW)
            xout[o - 1, t] = acc[:, at] + jnp.dot(
                chunk, w_ref[rows_last, at], preferred_element_type=F32
            )
            x_copy(o, t).start()
    for t in range(nt):
        at = pl.ds(pl.multiple_of(e * CW + t * TW, TW), TW)
        acc[:, at] += jnp.dot(chunk, w_ref[rows_last, at], preferred_element_type=F32)
    for t in range(nt):
        at = pl.ds(pl.multiple_of(e * CW + t * TW, TW), TW)
        whole = acc[:, at]
        for o in range(1, nh):
            x_copy(o, t).wait_recv()
            whole = whole + xin[o - 1, t]
        out_ref[:, t * TW : (t + 1) * TW] = whole.astype(BF16)

    for o in range(1, G):
        dec_copy(member(o), c).wait_send()
        for u in range(max(0, SUB - 2), SUB):
            mem_copy(member(o), c, u).wait_send()
        for u in range(SUB):
            pre_copy(member(o), c, u).wait_send()
    for o in range(1, nh):
        for t in range(nt):
            x_copy(o, t).wait_send()

    @pl.when(g < NG - 1)
    def _():
        for u in range(SUB):
            chain_copy(u).wait_send()


def solution(mesh):
    n, nh = mesh.shape["seq"], mesh.shape["head"]

    def shards(queries, keys, values, log_decay, norm_gain, out_weight, steer_ids, steer_table):
        T, features = queries.shape
        heads = log_decay.shape[1]
        HD = features // heads
        width = out_weight.shape[1]
        CW = width // nh
        G = 4
        HS = heads // G
        hb = 1
        SUB = HS // hb
        nt = max(1, CW // 512)
        TW = CW // nt
        pad = (HS + 7) // 8 * 8
        DMA = pltpu.SemaphoreType.DMA
        return pl.pallas_call(
            functools.partial(kernel, n, nh, G, SUB, hb, nt),
            out_shape=jax.ShapeDtypeStruct((T, CW), BF16),
            in_specs=[pl.BlockSpec(memory_space=pltpu.HBM)] * 8,
            out_specs=pl.BlockSpec(memory_space=pltpu.VMEM),
            scratch_shapes=[
                pltpu.VMEM((T, features), BF16),
                pltpu.VMEM((T, features), BF16),
                pltpu.VMEM((T, features), BF16),
                pltpu.VMEM((heads, T), F32),
                pltpu.VMEM((1, features), F32),
                pltpu.VMEM((1, T), jnp.int32),
                pltpu.VMEM(steer_table.shape, BF16),
                DMA((7,)),
                pltpu.VMEM((features, width), BF16),
                pltpu.VMEM((G, SUB, hb, HD, HD), F32),
                pltpu.VMEM((G, pad, HD), F32),
                pltpu.VMEM((G, SUB, hb, HD, HD), F32),
                pltpu.VMEM((G, pad, HD), F32),
                pltpu.VMEM((SUB, hb, HD, HD), F32),
                pltpu.VMEM((SUB, hb, HD, HD), F32),
                pltpu.VMEM((G, SUB, hb, HD, HD), F32),
                pltpu.VMEM((G, SUB, hb, HD, HD), F32),
                pltpu.VMEM((heads, T, HD), F32),
                pltpu.VMEM((heads, T, HD), F32),
                pltpu.VMEM((T, width), F32),
                pltpu.VMEM((nh - 1, nt, T, TW), F32),
                pltpu.VMEM((nh - 1, nt, T, TW), F32),
                DMA((W_COPIES,)),
                DMA((G, SUB)), DMA((G, SUB)),
                DMA((G,)), DMA((G,)),
                DMA((SUB,)), DMA((SUB,)),
                DMA((G, SUB)), DMA((G, SUB)),
                DMA((nh - 1, nt)), DMA((nh - 1, nt)),
            ],
            compiler_params=pltpu.CompilerParams(
                collective_id=0, has_side_effects=True, vmem_limit_bytes=60 * 1024 * 1024
            ),
            cost_estimate=pl.CostEstimate(
                flops=2 * T * features * width,
                bytes_accessed=2 * features * width,
                transcendentals=T * T * heads,
            ),
        )(
            queries, keys, values, log_decay.T, norm_gain.reshape(1, features), out_weight,
            steer_ids.reshape(1, T), steer_table,
        )

    in_specs = (
        P("seq", "head"), P("seq", "head"), P("seq", "head"), P("seq", "head"),
        P("head"), P("head", None), P("seq"), P(None, "head"),
    )
    return jax.shard_map(
        shards, mesh=mesh, in_specs=in_specs, out_specs=P("seq", "head"), check_vma=False
    )
```
